512 devices in a mesh: row: 16 (over x, y_hi, core), col: 32 (over y_lo, z).
Axes of the slice: x: 4, y: 4 (y_hi: 2, y_lo: 2; y = y_hi * 2 + y_lo), z: 16, core: 2. Of those that a mesh axis runs over, the one named last changes fastest.
Arguments:
- rhs: bfloat16 [49152, 8192], P('row', 'col'), may hold values from -6 to 6
- panel_columns: bfloat16 [2, 256, 49152], P(None, 'col', 'row'), may hold values from -0.375 to 0.375
- diag_inverse: float32 [2, 256, 256], replicated, may hold values from -2 to 2, as said below
- block_order: int32 [192], replicated, may hold values from 0 to 191, each once
Outputs:
- solved_rhs: bfloat16 [49152, 8192], P('row', 'col')
- gram: float32 [8192, 8192], P('row', 'col')
The draws below stay inside these ranges and needn't reach their ends.
Inputs may be any that keep to these rules, and one draw needn't show every extreme that they name: `diag_inverse`: each of the two matrices is lower triangular with a diagonal between 0.4 and 2.
All inputs are finite; a program needn't handle non-finite values.
Results may differ from the reference program's by a relative error of at most 0.0059.
Values may be sent and summed in bfloat16 or wider, within the bound.
A program may use at most 64 MiB of HBM per device.

```python
import math
import jax
import jax.numpy as jnp
from jax import lax

B = 256
NB = 192
ROWS = 49152
M = 8192


def draw_diag_inverse(key, part):
    key = jax.random.fold_in(key, 7)
    key_off, key_diag = jax.random.split(key)
    rows_idx = jnp.arange(B)[:, None]
    cols_idx = jnp.arange(B)[None, :]
    lower = (rows_idx > cols_idx)[None]
    unit = (rows_idx == cols_idx)[None].astype(jnp.float32)
    offdiag = jnp.clip(jax.random.normal(key_off, (2, B, B), jnp.float32), -4.0, 4.0)
    diagonal = jax.random.uniform(key_diag, (2, B), jnp.float32, 0.5, 1.5)
    scaled = jnp.where(lower, offdiag / math.sqrt(B), 0.0)
    return scaled + unit * diagonal[:, :, None]


def level_of(stream_key, extent, pieces, low, top_value):
    gain = 1.0
    for dim, parts in pieces:
        steps = jax.random.uniform(jax.random.fold_in(jax.random.fold_in(stream_key, 6), dim), (parts,), jnp.float32, low / len(pieces), top_value / len(pieces))
        gain = gain * jnp.repeat(jnp.exp(steps), extent[dim] // parts).reshape((-1,) + (1,) * (len(extent) - 1 - dim))
    return gain


def centred(rng, extent, deviation, limit, cuts=(), kind=jnp.bfloat16):
    result = jax.random.normal(rng, extent, jnp.float32) * deviation
    if len(cuts) > 0:
        result = level_of(rng, extent, cuts, -0.22, 0.18) * result
    return jnp.clip(result, min=-limit, max=limit).astype(kind)


def setup_inputs(seed: int = 0) -> dict:
    key_of = jax.random.split(jax.random.key(seed), 5)
    return {
        "rhs": centred(key_of[0], (ROWS, M), 1.0, 6.0, ((0, 16), (1, 32))),
        "panel_columns": centred(key_of[1], (2, B, ROWS), B ** -0.5, 0.375, ((1, 32), (2, 16))),
        "diag_inverse": draw_diag_inverse(jax.random.fold_in(key_of[4], 71), 0),
        "block_order": jax.random.permutation(key_of[3], NB).astype(jnp.int32),
    }


def reference(rhs, panel_columns, diag_inverse, block_order):
    block = diag_inverse.shape[1]
    nblocks = rhs.shape[0] // block
    width = rhs.shape[1]
    block_ids = jnp.arange(nblocks, dtype=jnp.int32)
    first = jnp.argmax(block_order == 0).astype(jnp.int32)
    second = jnp.argmax(block_order == 1).astype(jnp.int32)

    def solve(work, step, position):
        target = lax.dynamic_slice_in_dim(work, position * block, block, 0).astype(jnp.float32)
        product = jnp.dot(diag_inverse[step], target, precision=lax.Precision.HIGHEST, preferred_element_type=jnp.float32)
        return product.astype(jnp.bfloat16)

    def update(work, step, solved, active):
        blocks = work.reshape(nblocks, block, width)
        columns = panel_columns[step].reshape(block, nblocks, block).transpose(1, 0, 2)

        def one_block(items):
            current, factor, flag = items
            change = lax.dot_general(factor, solved, (((0,), (0,)), ((), ())), preferred_element_type=jnp.float32)
            fresh = (current.astype(jnp.float32) - change).astype(jnp.bfloat16)
            return jnp.where(flag, fresh, current)

        return lax.map(one_block, (blocks, columns, active)).reshape(nblocks * block, width)

    def place(work, solved, position):
        blocks = work.reshape(nblocks, block, width)
        hit = (block_ids == position)[:, None, None]
        return jnp.where(hit, solved[None], blocks).reshape(nblocks * block, width)

    first_block = solve(rhs, 0, first)
    work = update(rhs, 0, first_block, block_ids != first)
    work = place(work, first_block, first)
    second_block = solve(work, 1, second)
    work = update(work, 1, second_block, (block_ids != first) & (block_ids != second))
    work = place(work, second_block, second)
    finished = jnp.concatenate([first_block, second_block], 0)
    gram = lax.dot_general(finished, finished, (((0,), (0,)), ((), ())), preferred_element_type=jnp.float32) / (2 * block)
    return work, gram
```

```python
import jax
import jax.numpy as jnp
from jax import lax
from jax.experimental import pallas as pl
from jax.experimental.pallas import tpu as pltpu
from jax.sharding import PartitionSpec as P

MESH = pl.DeviceIdType.MESH
BLOCK = 256
ZN = 16
CHUNKS = 3
STREAMS = 4
LAST = ((0, 1), (2, 3))


def positions(order):
    places = lax.broadcasted_iota(jnp.int32, order.shape, 1)
    first = jnp.sum(jnp.where(order == 0, places, 0))
    second = jnp.sum(jnp.where(order == 1, places, 0))
    return first, second


def prepare(order_ref, rhs_ref, panel_ref, cand, blocks, factor_v, sem):
    row = lax.axis_index("row")
    nblocks = rhs_ref.shape[0] // BLOCK
    found = positions(order_ref[...])
    copies = []
    for b, place in enumerate(found):
        rows = pl.ds(pl.multiple_of((place % nblocks) * BLOCK, BLOCK), BLOCK)
        copies.append(pltpu.make_async_copy(rhs_ref.at[rows], blocks.at[b], sem.at[b]))
        if b == 1:
            copies.append(pltpu.make_async_copy(panel_ref.at[:, rows], factor_v, sem.at[2]))
    for copy in copies:
        copy.start()
    for copy in copies:
        copy.wait()
    owners = [place // nblocks == row for place in found]
    for b in range(2):
        block = jnp.where(owners[b], blocks[b], jnp.zeros_like(blocks[b]))
        for g in range(2):
            for part in range(2):
                cand[g * 4 + b * 2 + part, 0:128, :] = block[128 * part : 128 * part + 128, 128 * g : 128 * g + 128]
    factor = factor_v[...].astype(jnp.float32)[0:8]
    factor = jnp.where(owners[1], factor, jnp.zeros_like(factor))
    factor = jnp.concatenate([factor[:, 0:128], factor[:, 128:256]], 0).astype(cand.dtype)
    for part in range(8):
        cand[part, 128:144, :] = factor


def exchange(
    cand, piece_ref, g_ref, x_ref, ag_ref,
    rs, ys, yr, total,
    local_sem, rs_send, rs_recv, yx_sem, ag_send, ag_recv, t_sem,
    g_send, g_recv, beta_sem, y_send, y_recv, x_send, x_recv, xy_sem,
):
    row = lax.axis_index("row")
    col = lax.axis_index("col")
    x, yhi, core = row // 4, (row // 2) % 2, row % 2
    ylo, z = col // ZN, col % ZN
    q = x * 2 + core
    width = g_ref.shape[3]
    local = pltpu.make_async_copy

    def at(r, c):
        return {"row": r, "col": c}

    def remote(src, dst, send, recv, device):
        return pltpu.make_async_remote_copy(
            src_ref=src, dst_ref=dst, send_sem=send, recv_sem=recv, device_id=device, device_id_type=MESH
        )

    def peer(offset):
        other = (q + offset) % 8
        return (other // 2) * 4 + yhi * 2 + other % 2

    hi_partner = at(x * 4 + (1 - yhi) * 2 + core, col)
    lo_partner = at(row, (1 - ylo) * ZN + z)
    ring = (at(row, ylo * ZN + (z + 1) % ZN), at(row, ylo * ZN + (z + ZN - 1) % ZN))
    t_row, t_col = col // 2, 2 * row + col % 2
    t_partner = at(t_row, t_col)
    t_self = jnp.logical_and(t_row == row, t_col == col)

    barrier = pltpu.get_barrier_semaphore()

    def greet(device):
        pl.semaphore_signal(barrier, inc=1, device_id=device, device_id_type=MESH)

    for offset in range(1, 8):
        greet(at(peer(offset), col))
    for device in (hi_partner, lo_partner) + ring:
        greet(device)

    @pl.when(jnp.logical_not(t_self))
    def _():
        greet(t_partner)

    pl.semaphore_wait(barrier, 11 + jnp.where(t_self, 0, 1))

    def origin(direction, hops):
        return (z + (ZN - hops if direction == 0 else hops)) % ZN

    def held(stream, place):
        plane = ylo if stream < 3 else 1 - ylo
        return g_ref.at[min(stream, 2), plane * ZN + place]

    def own(chunk):
        return piece_ref.at[:, pl.ds(chunk * width, width)]

    def hop(direction, step, stream):
        place = origin(direction, step - 1)
        dst = held(stream, place)
        src = own(stream) if step == 1 and stream < 3 else dst
        return remote(
            src, dst, g_send.at[direction, step, stream], g_recv.at[direction, step, stream], ring[direction]
        )

    def landed(direction, step, stream):
        dst = held(stream, origin(direction, step))
        remote(
            dst, dst, g_send.at[direction, step, stream], g_recv.at[direction, step, stream], ring[direction]
        ).wait_recv()

    def across(place, chunk):
        dst = g_ref.at[chunk, ylo * ZN + place]
        offset = (place + ZN - z) % ZN
        return remote(dst, dst, y_send.at[offset, chunk], y_recv.at[offset, chunk], lo_partner)

    def across_landed(offset, chunk):
        dst = g_ref.at[chunk, (1 - ylo) * ZN + (z + offset) % ZN]
        remote(dst, dst, y_send.at[offset, chunk], y_recv.at[offset, chunk], lo_partner).wait_recv()

    def streams(direction, step):
        if step < 8:
            return range(STREAMS)
        return LAST[direction] if step == 8 else ()

    beta = remote(own(2), held(2, z), beta_sem.at[0], beta_sem.at[1], lo_partner)
    beta.start()
    for stream in range(3):
        for direction in range(2):
            hop(direction, 1, stream).start()
    for chunk in range(2):
        dst = g_ref.at[chunk, ylo * ZN + z]
        remote(own(chunk), dst, y_send.at[0, chunk], y_recv.at[0, chunk], lo_partner).start()
    keeps = [local(own(chunk), held(chunk, z), local_sem.at[2 + chunk]) for chunk in range(3)]
    for keep in keeps:
        keep.start()

    def scatter(offset):
        other = (q + offset) % 8
        return remote(cand.at[other], rs.at[q], rs_send.at[offset], rs_recv.at[offset], at(peer(offset), col))

    for offset in range(1, 8):
        scatter(offset).start()

    held_beta = held(3, z)
    remote(held_beta, held_beta, beta_sem.at[0], beta_sem.at[1], lo_partner).wait_recv()
    for direction in range(2):
        hop(direction, 1, 3).start()

    def ring_step(step):
        for stream in range(STREAMS):
            for direction in range(2):
                if stream not in streams(direction, step):
                    continue
                landed(direction, step, stream)
                if stream in streams(direction, step + 1):
                    hop(direction, step + 1, stream).start()
                if stream < 2:
                    across(origin(direction, step), stream).start()

    ring_step(1)

    for offset in range(1, 8):
        dst = rs.at[(q + 8 - offset) % 8]
        remote(dst, dst, rs_send.at[offset], rs_recv.at[offset], hi_partner).wait_recv()
    rs[q] = cand[q]
    summed = rs[0].astype(jnp.float32)
    for part in range(1, 8):
        summed = summed + rs[part].astype(jnp.float32)
    ys[...] = summed.astype(ys.dtype)
    swap = remote(ys, yr, yx_sem.at[0], yx_sem.at[1], hi_partner)
    swap.start()

    ring_step(2)

    swap.wait_recv()
    total[...] = (ys[...].astype(jnp.float32) + yr[...].astype(jnp.float32)).astype(total.dtype)

    def gather(offset):
        return remote(
            total.at[pl.ds(0, 128)], ag_ref.at[q], ag_send.at[offset], ag_recv.at[offset], at(peer(offset), col)
        )

    mine = total.at[pl.ds(pl.multiple_of(yhi * 64, 64), 64)]

    def turned(direction_col):
        return x_ref.at[direction_col % ZN, direction_col // ZN, pl.ds(0, 64)]

    turn = remote(mine, turned(t_col), t_sem.at[0], t_sem.at[1], t_partner)
    stay = local(mine, turned(col), t_sem.at[0])

    @pl.when(t_self)
    def _():
        stay.start()

    @pl.when(jnp.logical_not(t_self))
    def _():
        turn.start()

    corner = local(total.at[pl.ds(128, 16)], x_ref.at[z, ylo, pl.ds(64, 16)], local_sem.at[5])
    corner.start()
    for offset in range(1, 8):
        gather(offset).start()
    keep_slice = local(total.at[pl.ds(0, 128)], ag_ref.at[q], local_sem.at[6])
    keep_slice.start()

    ring_step(3)

    @pl.when(t_self)
    def _():
        stay.wait()

    @pl.when(jnp.logical_not(t_self))
    def _():
        dst = turned(col)
        remote(dst, dst, t_sem.at[0], t_sem.at[1], t_partner).wait_recv()
        turn.wait_send()

    corner.wait()
    x_mine, x_other = x_ref.at[z, ylo], x_ref.at[z, 1 - ylo]
    x_swap = remote(x_mine, x_mine, xy_sem.at[0], xy_sem.at[1], lo_partner)
    x_swap.start()

    ring_step(4)

    def x_held(direction, step, place):
        return x_ref.at[place] if step < 8 else x_ref.at[place, direction]

    def x_hop(direction, step):
        ref = x_held(direction, step, origin(direction, step - 1))
        return remote(ref, ref, x_send.at[direction, step], x_recv.at[direction, step], ring[direction])

    def x_step(step):
        for direction in range(2):
            ref = x_held(direction, step, origin(direction, step))
            remote(ref, ref, x_send.at[direction, step], x_recv.at[direction, step], ring[direction]).wait_recv()
            if step < 8:
                x_hop(direction, step + 1).start()

    remote(x_other, x_other, xy_sem.at[0], xy_sem.at[1], lo_partner).wait_recv()
    for direction in range(2):
        x_hop(direction, 1).start()
    ring_step(5)
    x_step(1)
    ring_step(6)
    x_step(2)
    ring_step(7)
    x_step(3)
    ring_step(8)
    for step in range(4, 9):
        x_step(step)

    for offset in range(1, 8):
        dst = ag_ref.at[(q + 8 - offset) % 8]
        remote(dst, dst, ag_send.at[offset], ag_recv.at[offset], hi_partner).wait_recv()
    for offset in range(ZN):
        for chunk in range(2):
            across_landed(offset, chunk)
    for keep in keeps:
        keep.wait()
    keep_slice.wait()
    beta.wait_send()
    swap.wait_send()
    x_swap.wait_send()
    for offset in range(1, 8):
        scatter(offset).wait_send()
        gather(offset).wait_send()
    for offset in range(ZN):
        for chunk in range(2):
            across((z + offset) % ZN, chunk).wait_send()
    for step in range(1, 9):
        for direction in range(2):
            for stream in streams(direction, step):
                hop(direction, step, stream).wait_send()
            x_hop(direction, step).wait_send()


def split3(value):
    parts = []
    for _ in range(3):
        part = value.astype(jnp.bfloat16)
        parts.append(part)
        value = value - part.astype(jnp.float32)
    return parts


def times(matrix, value):
    return sum(jnp.dot(part, value, preferred_element_type=jnp.float32) for part in reversed(split3(matrix)))


def contract_rows(a, b):
    return lax.dot_general(a, b, (((0,), (0,)), ((), ())), preferred_element_type=jnp.float32)


def compute(order_ref, diag_ref, x_ref, ag_ref, g_ref, rhs_ref, work_ref, gram_ref, solved, stacked, spots):
    step = pl.program_id(0)
    tile = rhs_ref.shape[0]
    per_tile = tile // BLOCK
    nblocks = per_tile * pl.num_programs(0)

    @pl.when(step == 0)
    def _():
        first, second = positions(order_ref[...])
        spots[0] = first
        spots[1] = second

        def columns(b):
            sides = [jnp.concatenate([ag_ref[g * 4 + b * 2], ag_ref[g * 4 + b * 2 + 1]], 0) for g in range(2)]
            for parity in range(2):
                for g in range(2):
                    rows = []
                    for core in range(2):
                        for yhi in range(2):
                            c = 2 * ((g * 2 + b) * 4 + yhi * 2 + core) + parity
                            rows.append(x_ref[c % ZN, c // ZN, 0:64])
                    sides.append(jnp.concatenate(rows, 0))
            return jnp.concatenate(sides, 1)

        corner = jnp.concatenate(
            [
                jnp.concatenate(
                    [x_ref[c % ZN, c // ZN, 64:80].astype(jnp.float32)[8 * g : 8 * g + 8] for c in range(2 * ZN)], 0
                )
                for g in range(2)
            ],
            1,
        ).astype(jnp.bfloat16)
        v0 = times(diag_ref[0], columns(0)).astype(jnp.bfloat16)
        left = (columns(1).astype(jnp.float32) - contract_rows(corner, v0)).astype(jnp.bfloat16)
        v1 = times(diag_ref[1], left).astype(jnp.bfloat16)
        solved[0] = v0[:, 0:BLOCK]
        solved[1] = v1[:, 0:BLOCK]
        own0 = v0[:, 0:BLOCK].astype(jnp.float32).reshape(2 * ZN, 8, BLOCK)
        own1 = v1[:, 0:BLOCK].astype(jnp.float32).reshape(2 * ZN, 8, BLOCK)
        stacked[...] = jnp.concatenate([own0, own1], 1).reshape(2 * BLOCK, BLOCK).astype(jnp.bfloat16)
        everything = jnp.concatenate([v0[:, BLOCK:], v1[:, BLOCK:]], 0)
        finished = jnp.concatenate([v0[:, 0:BLOCK], v1[:, 0:BLOCK]], 0)
        gram_ref[...] = contract_rows(everything, finished) / (2 * BLOCK)

    panel = g_ref[0].reshape(2 * BLOCK, tile)
    change = contract_rows(panel, stacked[...])
    base = lax.axis_index("row") * nblocks + step * per_tile
    for part in range(per_tile):
        rows = pl.ds(part * BLOCK, BLOCK)
        fresh = (rhs_ref[rows, :].astype(jnp.float32) - change[part * BLOCK : (part + 1) * BLOCK]).astype(jnp.bfloat16)
        place = base + part
        fresh = jnp.where(place == spots[0], solved[0], fresh)
        work_ref[rows, :] = jnp.where(place == spots[1], solved[1], fresh)


def shards(rhs, panel_columns, diag_inverse, block_order):
    rows, width = rhs.shape
    order = block_order.reshape(1, -1)
    piece = panel_columns.reshape(16, rows)
    bf16 = jnp.bfloat16
    dma = pltpu.SemaphoreType.DMA
    any_space = pl.BlockSpec(memory_space=pl.ANY)
    in_vmem = pl.BlockSpec(memory_space=pltpu.VMEM)
    chunk = rows // CHUNKS
    cand = pl.pallas_call(
        prepare,
        name="prepare",
        out_shape=jax.ShapeDtypeStruct((8, 144, 128), bf16),
        in_specs=[in_vmem, any_space, any_space],
        out_specs=in_vmem,
        scratch_shapes=[pltpu.VMEM((2, BLOCK, width), bf16), pltpu.VMEM((16, BLOCK), bf16), dma((3,))],
        compiler_params=pltpu.CompilerParams(vmem_limit_bytes=60 * 1024 * 1024),
    )(order, rhs, piece)
    g, x, ag = pl.pallas_call(
        exchange,
        name="exchange",
        out_shape=(
            jax.ShapeDtypeStruct((CHUNKS, 2 * ZN, 16, chunk), bf16),
            jax.ShapeDtypeStruct((ZN, 2, 80, 128), bf16),
            jax.ShapeDtypeStruct((8, 128, 128), bf16),
        ),
        in_specs=[in_vmem, any_space],
        out_specs=(any_space, any_space, any_space),
        scratch_shapes=[
            pltpu.VMEM((8, 144, 128), bf16),
            pltpu.VMEM((144, 128), bf16),
            pltpu.VMEM((144, 128), bf16),
            pltpu.VMEM((144, 128), bf16),
            dma((7,)), dma((8,)), dma((8,)), dma((2,)), dma((8,)), dma((8,)), dma((2,)),
            dma((2, 9, STREAMS)), dma((2, 9, STREAMS)), dma((2,)), dma((ZN, 2)), dma((ZN, 2)),
            dma((2, 9)), dma((2, 9)), dma((2,)),
        ],
        compiler_params=pltpu.CompilerParams(
            collective_id=0, has_side_effects=True, vmem_limit_bytes=32 * 1024 * 1024
        ),
    )(cand, piece)
    span = width * 32 // 16
    tile = 512
    fixed = lambda rank: (lambda i: (0,) * rank)
    per_chunk = chunk // tile
    work, gram = pl.pallas_call(
        compute,
        name="compute",
        grid=(rows // tile,),
        out_shape=(
            jax.ShapeDtypeStruct((rows, width), bf16),
            jax.ShapeDtypeStruct((span, width), jnp.float32),
        ),
        in_specs=[
            pl.BlockSpec((1, order.shape[1]), fixed(2)),
            pl.BlockSpec(diag_inverse.shape, fixed(3)),
            pl.BlockSpec(x.shape, fixed(4)),
            pl.BlockSpec(ag.shape, fixed(3)),
            pl.BlockSpec((1, 2 * ZN, 16, tile), lambda i: (i // per_chunk, 0, 0, i % per_chunk)),
            pl.BlockSpec((tile, width), lambda i: (i, 0)),
        ],
        out_specs=(
            pl.BlockSpec((tile, width), lambda i: (i, 0)),
            pl.BlockSpec((span, width), fixed(2)),
        ),
        scratch_shapes=[
            pltpu.VMEM((2, BLOCK, width), bf16),
            pltpu.VMEM((2 * BLOCK, width), bf16),
            pltpu.SMEM((2,), jnp.int32),
        ],
        compiler_params=pltpu.CompilerParams(vmem_limit_bytes=32 * 1024 * 1024),
    )(order, diag_inverse, x, ag, g, rhs)
    return work, gram


def solution(mesh):
    in_specs = (P("row", "col"), P(None, "col", "row"), P(), P())
    out_specs = (P("row", "col"), P("row", "col"))
    return jax.shard_map(shards, mesh=mesh, in_specs=in_specs, out_specs=out_specs, check_vma=False)
```

```python
import jax
import jax.numpy as jnp
from jax import lax
from jax.experimental import pallas as pl
from jax.experimental.pallas import tpu as pltpu
from jax.sharding import PartitionSpec as P

MESH = pl.DeviceIdType.MESH
BLOCK = 256
ZN = 16
RN = 16
NEAR, FAR, OTHER, EXTRA = range(4)
STREAMS = (NEAR, FAR, OTHER)
LAST = ((NEAR, EXTRA), (FAR, OTHER))
ADD_AT = 2
EXTRA_AT = 6
EXTRA_EVERY = 2


def exchange(
    order_ref, rhs_ref, piece_ref, g_ref, x_ref, ag_ref,
    rhs_v, panel_v, cand, rs, total,
    local_sem, rs_send, rs_recv, ag_send, ag_recv, t_sem,
    g_send, g_recv, beta_sem, y_send, y_recv,
):
    row = lax.axis_index("row")
    col = lax.axis_index("col")
    ylo, z = col // ZN, col % ZN
    nblocks = rhs_ref.shape[0] // BLOCK
    width = g_ref.shape[3]
    local = pltpu.make_async_copy

    def at(r, c):
        return {"row": r, "col": c}

    def remote(src, dst, send, recv, device):
        return pltpu.make_async_remote_copy(
            src_ref=src, dst_ref=dst, send_sem=send, recv_sem=recv, device_id=device, device_id_type=MESH
        )

    def peer(offset):
        return at((row + offset) % RN, col)

    lo_partner = at(row, (1 - ylo) * ZN + z)
    ring = (at(row, ylo * ZN + (z + 1) % ZN), at(row, ylo * ZN + (z + ZN - 1) % ZN))
    t_row, t_col = col // 2, 2 * row + col % 2
    t_partner = at(t_row, t_col)
    t_self = jnp.logical_and(t_row == row, t_col == col)

    rhs_in = local(rhs_ref, rhs_v, local_sem.at[0])
    panel_in = local(piece_ref, panel_v, local_sem.at[1])
    rhs_in.start()
    panel_in.start()

    barrier = pltpu.get_barrier_semaphore()

    def greet(device):
        pl.semaphore_signal(barrier, inc=1, device_id=device, device_id_type=MESH)

    for offset in range(1, RN):
        greet(peer(offset))
    for device in (lo_partner,) + ring:
        greet(device)

    @pl.when(jnp.logical_not(t_self))
    def _():
        greet(t_partner)

    pl.semaphore_wait(barrier, RN + 2 + jnp.where(t_self, 0, 1))

    def origin(direction, hops):
        return (z + (ZN - hops if direction == 0 else hops)) % ZN

    def held(stream, place):
        plane = 1 - ylo if stream == OTHER else ylo
        if stream == EXTRA:
            return x_ref.at[plane * ZN + place]
        return g_ref.at[0 if stream == NEAR else 1, plane * ZN + place]

    def own(stream):
        return piece_ref.at[:, pl.ds(stream * width, width)]

    def hop(direction, step, stream):
        dst = held(stream, origin(direction, step - 1))
        src = own(stream) if step == 1 and stream in (NEAR, FAR) else dst
        return remote(
            src, dst, g_send.at[direction, step, stream], g_recv.at[direction, step, stream], ring[direction]
        )

    def runs(direction, step, stream):
        return step < 8 or (step == 8 and stream in LAST[direction])

    def across(place, stream):
        dst = held(stream, place)
        src = own(stream) if stream == NEAR and place is z else dst
        offset = (place + ZN - z) % ZN
        return remote(src, dst, y_send.at[offset, stream // EXTRA], y_recv.at[offset, stream // EXTRA], lo_partner)

    def across_landed(offset, stream):
        place = (1 - ylo) * ZN + (z + offset) % ZN
        dst = x_ref.at[place] if stream == EXTRA else g_ref.at[0, place]
        remote(dst, dst, y_send.at[offset, stream // EXTRA], y_recv.at[offset, stream // EXTRA], lo_partner).wait_recv()

    def begin(stream):
        for direction in range(2):
            hop(direction, 1, stream).start()

    def turn_over(step, stream):
        for direction in range(2):
            if not runs(direction, step, stream):
                continue
            place = origin(direction, step)
            dst = held(stream, place)
            remote(
                dst, dst, g_send.at[direction, step, stream], g_recv.at[direction, step, stream], ring[direction]
            ).wait_recv()
            if runs(direction, step + 1, stream):
                hop(direction, step + 1, stream).start()
            if stream in (NEAR, EXTRA):
                across(place, stream).start()

    beta = remote(own(FAR), g_ref.at[1, ylo * ZN + z], beta_sem.at[0], beta_sem.at[1], lo_partner)
    beta.start()
    begin(NEAR)
    across(z, NEAR).start()

    rhs_in.wait()
    masks = [[(order_ref[row * nblocks + p] == b).astype(jnp.float32) for p in range(nblocks)] for b in range(2)]

    def masked(b):
        block = jnp.zeros((BLOCK, rhs_v.shape[1]), jnp.float32)
        for p in range(nblocks):
            block = block + rhs_v[pl.ds(p * BLOCK, BLOCK), :].astype(jnp.float32) * masks[b][p]
        block = block.astype(cand.dtype)
        for g in range(2):
            for part in range(4):
                cand[g * 8 + b * 4 + part, 0:64, :] = block[64 * part : 64 * part + 64, 128 * g : 128 * g + 128]

    masked(0)
    begin(FAR)
    masked(1)
    panel_in.wait()
    factor = jnp.zeros((8, BLOCK), jnp.float32)
    for p in range(nblocks):
        factor = factor + panel_v[:, pl.ds(p * BLOCK, BLOCK)].astype(jnp.float32)[0:8] * masks[1][p]
    factor = jnp.concatenate([factor[:, 0:128], factor[:, 128:256]], 0).astype(cand.dtype)
    for part in range(RN):
        cand[part, 64:80, :] = factor

    def scatter(offset):
        other = (row + offset) % RN
        return remote(cand.at[other], rs.at[row], rs_send.at[offset], rs_recv.at[offset], peer(offset))

    for offset in range(1, RN):
        scatter(offset).start()
    rs[row] = cand[row]
    keeps = [local(own(stream), held(stream, z), local_sem.at[2 + stream]) for stream in (NEAR, FAR)]
    for keep in keeps:
        keep.start()

    theirs = held(OTHER, z)
    remote(theirs, theirs, beta_sem.at[0], beta_sem.at[1], lo_partner).wait_recv()
    begin(OTHER)

    def gather(offset):
        return remote(total.at[pl.ds(0, 64)], ag_ref.at[row], ag_send.at[offset], ag_recv.at[offset], peer(offset))

    def slot(place):
        return x_ref.at[place, pl.ds(0, 64)]

    turn = remote(total.at[pl.ds(0, 64)], slot(t_col), t_sem.at[0], t_sem.at[1], t_partner)
    stay = local(total.at[pl.ds(0, 64)], slot(col), t_sem.at[0])
    corner = local(total.at[pl.ds(64, 16)], x_ref.at[col, pl.ds(64, 16)], local_sem.at[4])
    keep_slice = local(total.at[pl.ds(0, 64)], ag_ref.at[row], local_sem.at[5])

    def add_up():
        for offset in range(1, RN):
            dst = rs.at[(row + RN - offset) % RN]
            remote(dst, dst, rs_send.at[offset], rs_recv.at[offset], lo_partner).wait_recv()
        summed = rs[0].astype(jnp.float32)
        for part in range(1, RN):
            summed = summed + rs[part].astype(jnp.float32)
        total[...] = summed.astype(total.dtype)

        @pl.when(t_self)
        def _():
            stay.start()

        @pl.when(jnp.logical_not(t_self))
        def _():
            turn.start()

        corner.start()
        for offset in range(1, RN):
            gather(offset).start()
        keep_slice.start()

    def begin_extra():
        @pl.when(t_self)
        def _():
            stay.wait()

        @pl.when(jnp.logical_not(t_self))
        def _():
            dst = slot(col)
            remote(dst, dst, t_sem.at[0], t_sem.at[1], t_partner).wait_recv()
            turn.wait_send()

        corner.wait()
        begin(EXTRA)
        across(z, EXTRA).start()

    spot = 0
    extra = 0
    for step in range(1, 9):
        for stream in STREAMS:
            turn_over(step, stream)
            spot += 1
            if spot == ADD_AT:
                add_up()
            if spot == EXTRA_AT:
                begin_extra()
            if spot > EXTRA_AT and (spot - EXTRA_AT) % EXTRA_EVERY == 0 and extra < 8:
                extra += 1
                turn_over(extra, EXTRA)
    while extra < 8:
        extra += 1
        turn_over(extra, EXTRA)

    for offset in range(1, RN):
        dst = ag_ref.at[(row + RN - offset) % RN]
        remote(dst, dst, ag_send.at[offset], ag_recv.at[offset], lo_partner).wait_recv()
    for offset in range(ZN):
        for stream in (NEAR, EXTRA):
            across_landed(offset, stream)
    for keep in keeps:
        keep.wait()
    keep_slice.wait()
    beta.wait_send()
    for offset in range(1, RN):
        scatter(offset).wait_send()
        gather(offset).wait_send()
    for offset in range(ZN):
        for stream in (NEAR, EXTRA):
            across((z + offset) % ZN, stream).wait_send()
    for step in range(1, 9):
        for direction in range(2):
            for stream in STREAMS + (EXTRA,):
                if runs(direction, step, stream):
                    hop(direction, step, stream).wait_send()


def split3(value):
    parts = []
    for _ in range(3):
        part = value.astype(jnp.bfloat16)
        parts.append(part)
        value = value - part.astype(jnp.float32)
    return parts


def times(matrix, value):
    return sum(jnp.dot(part, value, preferred_element_type=jnp.float32) for part in reversed(split3(matrix)))


def contract_rows(a, b):
    return lax.dot_general(a, b, (((0,), (0,)), ((), ())), preferred_element_type=jnp.float32)


def compute(order_ref, diag_ref, x_ref, ag_ref, g_ref, rhs_ref, work_ref, gram_ref, solved, stacked):
    step = pl.program_id(0)
    tile = rhs_ref.shape[0]
    per_tile = tile // BLOCK
    nblocks = per_tile * pl.num_programs(0)

    @pl.when(step == 0)
    def _():

        def columns(b):
            sides = [jnp.concatenate([ag_ref[g * 8 + b * 4 + part] for part in range(4)], 0) for g in range(2)]
            for parity in range(2):
                for g in range(2):
                    sides.append(
                        jnp.concatenate([x_ref[2 * (g * 8 + b * 4 + part) + parity, 0:64] for part in range(4)], 0)
                    )
            return jnp.concatenate(sides, 1)

        corner = jnp.concatenate(
            [
                jnp.concatenate(
                    [x_ref[c, 64:80].astype(jnp.float32)[8 * g : 8 * g + 8] for c in range(2 * ZN)], 0
                )
                for g in range(2)
            ],
            1,
        ).astype(jnp.bfloat16)
        v0 = times(diag_ref[0], columns(0)).astype(jnp.bfloat16)
        left = (columns(1).astype(jnp.float32) - contract_rows(corner, v0)).astype(jnp.bfloat16)
        v1 = times(diag_ref[1], left).astype(jnp.bfloat16)
        solved[0] = v0[:, 0:BLOCK]
        solved[1] = v1[:, 0:BLOCK]
        own0 = v0[:, 0:BLOCK].astype(jnp.float32).reshape(2 * ZN, 8, BLOCK)
        own1 = v1[:, 0:BLOCK].astype(jnp.float32).reshape(2 * ZN, 8, BLOCK)
        stacked[...] = jnp.concatenate([own0, own1], 1).reshape(2 * BLOCK, BLOCK).astype(jnp.bfloat16)
        everything = jnp.concatenate([v0[:, BLOCK:], v1[:, BLOCK:]], 0)
        finished = jnp.concatenate([v0[:, 0:BLOCK], v1[:, 0:BLOCK]], 0)
        gram_ref[...] = contract_rows(everything, finished) / (2 * BLOCK)

    panel = g_ref[0].reshape(2 * BLOCK, tile)
    change = contract_rows(panel, stacked[...])
    base = lax.axis_index("row") * nblocks + step * per_tile
    for part in range(per_tile):
        rows = pl.ds(part * BLOCK, BLOCK)
        fresh = (rhs_ref[rows, :].astype(jnp.float32) - change[part * BLOCK : (part + 1) * BLOCK]).astype(jnp.bfloat16)
        which = order_ref[base + part]
        fresh = jnp.where(which == 0, solved[0], fresh)
        work_ref[rows, :] = jnp.where(which == 1, solved[1], fresh)


def shards(rhs, panel_columns, diag_inverse, block_order):
    rows, width = rhs.shape
    piece = panel_columns.reshape(16, rows)
    bf16 = jnp.bfloat16
    dma = pltpu.SemaphoreType.DMA
    any_space = pl.BlockSpec(memory_space=pl.ANY)
    in_smem = pl.BlockSpec(memory_space=pltpu.SMEM)
    chunk = rows // 2
    g, x, ag = pl.pallas_call(
        exchange,
        name="exchange",
        out_shape=(
            jax.ShapeDtypeStruct((2, 2 * ZN, 16, chunk), bf16),
            jax.ShapeDtypeStruct((2 * ZN, 80, 128), bf16),
            jax.ShapeDtypeStruct((RN, 64, 128), bf16),
        ),
        in_specs=[in_smem, any_space, any_space],
        out_specs=(any_space, any_space, any_space),
        scratch_shapes=[
            pltpu.VMEM((rows, width), bf16),
            pltpu.VMEM((16, rows), bf16),
            pltpu.VMEM((RN, 80, 128), bf16),
            pltpu.VMEM((RN, 80, 128), bf16),
            pltpu.VMEM((80, 128), bf16),
            dma((6,)), dma((RN,)), dma((RN,)), dma((RN,)), dma((RN,)), dma((2,)),
            dma((2, 9, 4)), dma((2, 9, 4)), dma((2,)), dma((ZN, 2)), dma((ZN, 2)),
        ],
        compiler_params=pltpu.CompilerParams(
            collective_id=0, has_side_effects=True, vmem_limit_bytes=32 * 1024 * 1024
        ),
    )(block_order, rhs, piece)
    span = width * 32 // 16
    tile = 512
    fixed = lambda rank: (lambda i: (0,) * rank)
    per_chunk = chunk // tile
    work, gram = pl.pallas_call(
        compute,
        name="compute",
        grid=(rows // tile,),
        out_shape=(
            jax.ShapeDtypeStruct((rows, width), bf16),
            jax.ShapeDtypeStruct((span, width), jnp.float32),
        ),
        in_specs=[
            in_smem,
            pl.BlockSpec(diag_inverse.shape, fixed(3)),
            pl.BlockSpec(x.shape, fixed(3)),
            pl.BlockSpec(ag.shape, fixed(3)),
            pl.BlockSpec((1, 2 * ZN, 16, tile), lambda i: (i // per_chunk, 0, 0, i % per_chunk)),
            pl.BlockSpec((tile, width), lambda i: (i, 0)),
        ],
        out_specs=(
            pl.BlockSpec((tile, width), lambda i: (i, 0)),
            pl.BlockSpec((span, width), fixed(2)),
        ),
        scratch_shapes=[
            pltpu.VMEM((2, BLOCK, width), bf16),
            pltpu.VMEM((2 * BLOCK, width), bf16),
        ],
        compiler_params=pltpu.CompilerParams(vmem_limit_bytes=32 * 1024 * 1024),
    )(block_order, diag_inverse, x, ag, g, rhs)
    return work, gram


def solution(mesh):
    in_specs = (P("row", "col"), P(None, "col", "row"), P(), P())
    out_specs = (P("row", "col"), P("row", "col"))
    return jax.shard_map(shards, mesh=mesh, in_specs=in_specs, out_specs=out_specs, check_vma=False)
```

```python
import functools

import jax
import jax.numpy as jnp
from jax import lax
from jax.experimental import pallas as pl
from jax.experimental.pallas import tpu as pltpu
from jax.sharding import PartitionSpec as P

MESH = pl.DeviceIdType.MESH
BLOCK = 256
ZN = 16
RN = 16
NEAR, FAR, OTHER = STREAMS = range(3)
LAST = ((NEAR,), (FAR, OTHER))
STEP = 4.1
FIRST = {NEAR: 3.5, FAR: 4.5, OTHER: 6.0}
ADD_AT = 9.5
EXTRA_AT = 17.0
EXTRA_STEP = 5.0
SOLVE_AT = 33.0
REACH = 4
TILE = 512


def split3(value):
    parts = []
    for _ in range(3):
        part = value.astype(jnp.bfloat16)
        parts.append(part)
        value = value - part.astype(jnp.float32)
    return parts


def times(matrix, value):
    return sum(jnp.dot(part, value, preferred_element_type=jnp.float32) for part in reversed(split3(matrix)))


def contract_rows(a, b):
    return lax.dot_general(a, b, (((0,), (0,)), ((), ())), preferred_element_type=jnp.float32)


def whole(
    order_ref, diag_ref, rhs_ref, piece_ref, work_ref, gram_ref,
    rhs_v, panel_v, diag_v, g_ref, x_ref, ag_ref, cand, rs, total, solved, stacked, work_v, gram_v,
    local_sem, rs_send, rs_recv, ag_send, ag_recv, t_sem,
    g_send, g_recv, beta_sem, y_send, y_recv, x_send, x_recv, out_sem,
):
    row = lax.axis_index("row")
    col = lax.axis_index("col")
    ylo, z = col // ZN, col % ZN
    nblocks = rhs_ref.shape[0] // BLOCK
    width = g_ref.shape[3]
    local = pltpu.make_async_copy

    def at(r, c):
        return {"row": r, "col": c}

    def remote(src, dst, send, recv, device):
        return pltpu.make_async_remote_copy(
            src_ref=src, dst_ref=dst, send_sem=send, recv_sem=recv, device_id=device, device_id_type=MESH
        )

    def peer(offset):
        return at((row + offset) % RN, col)

    lo_partner = at(row, (1 - ylo) * ZN + z)
    ring = (at(row, ylo * ZN + (z + 1) % ZN), at(row, ylo * ZN + (z + ZN - 1) % ZN))
    reaches = [
        (at(row, ylo * ZN + (z + far) % ZN), at(row, ylo * ZN + (z + ZN - far) % ZN)) for far in range(1, REACH + 1)
    ]
    t_row, t_col = col // 2, 2 * row + col % 2
    t_partner = at(t_row, t_col)
    t_self = jnp.logical_and(t_row == row, t_col == col)

    rhs_in = local(rhs_ref, rhs_v, local_sem.at[0])
    panel_in = local(piece_ref, panel_v, local_sem.at[1])
    rhs_in.start()
    panel_in.start()
    diag_in = local(diag_ref, diag_v, local_sem.at[6])
    diag_in.start()

    barrier = pltpu.get_barrier_semaphore()

    def greet(device):
        pl.semaphore_signal(barrier, inc=1, device_id=device, device_id_type=MESH)

    for offset in range(1, RN):
        greet(peer(offset))
    greet(lo_partner)
    for pair in reaches:
        for device in pair:
            greet(device)

    @pl.when(jnp.logical_not(t_self))
    def _():
        greet(t_partner)

    pl.semaphore_wait(barrier, RN + 2 * REACH + jnp.where(t_self, 0, 1))

    def origin(direction, hops):
        return (z + (ZN - hops if direction == 0 else hops)) % ZN

    def held(stream, place):
        plane = 1 - ylo if stream == OTHER else ylo
        return g_ref.at[0 if stream == NEAR else 1, plane * ZN + place]

    def own(stream):
        return piece_ref.at[:, pl.ds(stream * width, width)]

    def hop(direction, step, stream):
        dst = held(stream, origin(direction, step - 1))
        src = own(stream) if step == 1 and stream in (NEAR, FAR) else dst
        return remote(
            src, dst, g_send.at[direction, step, stream], g_recv.at[direction, step, stream], ring[direction]
        )

    def runs(direction, step, stream):
        return step < 8 or (step == 8 and stream in LAST[direction])

    def across(place, extra):
        place_in_col = ylo * ZN + place
        dst = x_ref.at[place_in_col] if extra else g_ref.at[0, place_in_col]
        offset = (place + ZN - z) % ZN
        return remote(dst, dst, y_send.at[offset, extra], y_recv.at[offset, extra], lo_partner)

    def across_landed(offset, extra):
        place_in_col = (1 - ylo) * ZN + (z + offset) % ZN
        dst = x_ref.at[place_in_col] if extra else g_ref.at[0, place_in_col]
        remote(dst, dst, y_send.at[offset, extra], y_recv.at[offset, extra], lo_partner).wait_recv()

    def begin(stream):
        for direction in range(2):
            hop(direction, 1, stream).start()

    def turn_over(step, stream):
        for direction in range(2):
            if not runs(direction, step, stream):
                continue
            place = origin(direction, step)
            dst = held(stream, place)
            remote(
                dst, dst, g_send.at[direction, step, stream], g_recv.at[direction, step, stream], ring[direction]
            ).wait_recv()
            if runs(direction, step + 1, stream):
                hop(direction, step + 1, stream).start()
            if stream == NEAR:
                across(place, 0).start()

    def x_far(direction, hops):
        return range(hops + 1, min(hops + REACH, 7 + (direction == 0)) + 1)

    def x_hop(direction, hops, reach):
        dst = x_ref.at[ylo * ZN + origin(direction, hops)]
        to = reaches[reach - hops - 1][direction]
        return remote(dst, dst, x_send.at[direction, reach], x_recv.at[direction, reach], to)

    def x_begin(hops):
        for reach in range(hops + REACH, hops, -1):
            for direction in range(2):
                if reach in x_far(direction, hops):
                    x_hop(direction, hops, reach).start()

    def x_landed(hops):
        for direction in range(2):
            if hops <= 7 + (direction == 0):
                dst = x_ref.at[ylo * ZN + origin(direction, hops)]
                remote(
                    dst, dst, x_send.at[direction, hops], x_recv.at[direction, hops], ring[direction]
                ).wait_recv()
                if hops == REACH:
                    for reach in reversed(x_far(direction, hops)):
                        x_hop(direction, hops, reach).start()
                across(origin(direction, hops), 1).start()

    beta = remote(own(FAR), g_ref.at[1, ylo * ZN + z], beta_sem.at[0], beta_sem.at[1], lo_partner)
    beta.start()
    begin(NEAR)
    begin(FAR)
    remote(own(NEAR), held(NEAR, z), y_send.at[0, 0], y_recv.at[0, 0], lo_partner).start()

    rhs_in.wait()
    masks = [[(order_ref[row * nblocks + p] == b).astype(jnp.float32) for p in range(nblocks)] for b in range(2)]

    def masked(part, carry):
        for g in range(2):
            lanes = pl.ds(128 * g, 128)
            sums = [jnp.zeros((64, 128), jnp.float32)] * 2
            for p in range(nblocks):
                rows = pl.ds(pl.multiple_of(p * BLOCK + part * 64, 64), 64)
                value = rhs_v[rows, lanes].astype(jnp.float32)
                sums = [total_ + value * masks[b][p] for b, total_ in enumerate(sums)]
            for b in range(2):
                cand[g * 8 + b * 4 + part, 0:64, :] = sums[b].astype(cand.dtype)
        return carry

    lax.fori_loop(0, 4, masked, 0)
    panel_in.wait()
    factor = jnp.zeros((8, BLOCK), jnp.float32)
    for p in range(nblocks):
        factor = factor + panel_v[:, pl.ds(p * BLOCK, BLOCK)].astype(jnp.float32)[0:8] * masks[1][p]
    factor = jnp.concatenate([factor[:, 0:128], factor[:, 128:256]], 0).astype(cand.dtype)
    for part in range(RN):
        cand[part, 64:80, :] = factor

    def scatter(offset):
        other = (row + offset) % RN
        return remote(cand.at[other], rs.at[row], rs_send.at[offset], rs_recv.at[offset], peer(offset))

    for offset in range(1, RN):
        scatter(offset).start()
    rs[row] = cand[row]
    keeps = [local(own(stream), held(stream, z), local_sem.at[2 + stream]) for stream in (NEAR, FAR)]
    for keep in keeps:
        keep.start()

    theirs = held(OTHER, z)
    remote(theirs, theirs, beta_sem.at[0], beta_sem.at[1], lo_partner).wait_recv()
    begin(OTHER)

    def gather(offset):
        return remote(total.at[pl.ds(0, 64)], ag_ref.at[row], ag_send.at[offset], ag_recv.at[offset], peer(offset))

    def slot(place):
        return x_ref.at[place, pl.ds(0, 64)]

    turn = remote(total.at[pl.ds(0, 64)], slot(t_col), t_sem.at[0], t_sem.at[1], t_partner)
    stay = local(total.at[pl.ds(0, 64)], slot(col), t_sem.at[0])
    corner = local(total.at[pl.ds(64, 16)], x_ref.at[col, pl.ds(64, 16)], local_sem.at[4])
    keep_slice = local(total.at[pl.ds(0, 64)], ag_ref.at[row], local_sem.at[5])

    def add_up():
        for offset in range(1, RN):
            dst = rs.at[(row + RN - offset) % RN]
            remote(dst, dst, rs_send.at[offset], rs_recv.at[offset], lo_partner).wait_recv()
        summed = rs[0].astype(jnp.float32)
        for part in range(1, RN):
            summed = summed + rs[part].astype(jnp.float32)
        total[...] = summed.astype(total.dtype)

        @pl.when(t_self)
        def _():
            stay.start()

        @pl.when(jnp.logical_not(t_self))
        def _():
            turn.start()

        corner.start()
        for offset in range(1, RN):
            gather(offset).start()
        keep_slice.start()

    def begin_extra():
        @pl.when(t_self)
        def _():
            stay.wait()

        @pl.when(jnp.logical_not(t_self))
        def _():
            dst = slot(col)
            remote(dst, dst, t_sem.at[0], t_sem.at[1], t_partner).wait_recv()
            turn.wait_send()

        corner.wait()
        x_begin(0)
        across(z, 1).start()

    def solve():
        for offset in range(1, RN):
            dst = ag_ref.at[(row + RN - offset) % RN]
            remote(dst, dst, ag_send.at[offset], ag_recv.at[offset], lo_partner).wait_recv()
        keep_slice.wait()
        diag_in.wait()
        for offset in range(ZN):
            across_landed(offset, 1)

        def columns(b):
            sides = [jnp.concatenate([ag_ref[g * 8 + b * 4 + part] for part in range(4)], 0) for g in range(2)]
            for parity in range(2):
                for g in range(2):
                    sides.append(
                        jnp.concatenate([x_ref[2 * (g * 8 + b * 4 + part) + parity, 0:64] for part in range(4)], 0)
                    )
            return jnp.concatenate(sides, 1)

        corner_rows = jnp.concatenate(
            [
                jnp.concatenate([x_ref[c, 64:80].astype(jnp.float32)[8 * g : 8 * g + 8] for c in range(2 * ZN)], 0)
                for g in range(2)
            ],
            1,
        ).astype(jnp.bfloat16)
        v0 = times(diag_v[0], columns(0)).astype(jnp.bfloat16)
        left = (columns(1).astype(jnp.float32) - contract_rows(corner_rows, v0)).astype(jnp.bfloat16)
        v1 = times(diag_v[1], left).astype(jnp.bfloat16)
        solved[0] = v0[:, 0:BLOCK]
        solved[1] = v1[:, 0:BLOCK]
        own0 = v0[:, 0:BLOCK].astype(jnp.float32).reshape(2 * ZN, 8, BLOCK)
        own1 = v1[:, 0:BLOCK].astype(jnp.float32).reshape(2 * ZN, 8, BLOCK)
        stacked[...] = jnp.concatenate([own0, own1], 1).reshape(2 * BLOCK, BLOCK).astype(jnp.bfloat16)
        everything = jnp.concatenate([v0[:, BLOCK:], v1[:, BLOCK:]], 0)
        finished = jnp.concatenate([v0[:, 0:BLOCK], v1[:, 0:BLOCK]], 0)
        gram_v[...] = contract_rows(everything, finished) / (2 * BLOCK)

    def update(half):
        outs = []
        for tile in range(width // TILE):
            panel = g_ref[half, :, :, pl.ds(tile * TILE, TILE)].reshape(2 * BLOCK, TILE)
            change = contract_rows(panel, stacked[...])
            for part in range(TILE // BLOCK):
                p = half * (width // BLOCK) + tile * (TILE // BLOCK) + part
                rows = pl.ds(p * BLOCK, BLOCK)
                fresh = rhs_v[rows, :].astype(jnp.float32) - change[part * BLOCK : (part + 1) * BLOCK]
                fresh = fresh.astype(jnp.bfloat16)
                which = order_ref[row * nblocks + p]
                fresh = jnp.where(which == 0, solved[0], fresh)
                work_v[rows, :] = jnp.where(which == 1, solved[1], fresh)
            rows = pl.ds(half * width + tile * TILE, TILE)
            out = local(work_v.at[rows], work_ref.at[rows], out_sem.at[half * (width // TILE) + tile])
            out.start()
            outs.append(out)
        return outs

    outs = []

    def solve_and_write():
        solve()
        out = local(gram_v, gram_ref, out_sem.at[2 * (width // TILE)])
        out.start()
        outs.append(out)

    plan = [
        (FIRST[stream] + STEP * (step - 1), functools.partial(turn_over, step, stream))
        for step in range(1, 9)
        for stream in STREAMS
    ]
    plan += [(ADD_AT, add_up), (EXTRA_AT, begin_extra), (SOLVE_AT, solve_and_write)]
    plan += [
        (EXTRA_AT + EXTRA_STEP * (1 + (hops - 1) // REACH), functools.partial(x_landed, hops))
        for hops in (4, 1, 2, 3, 8, 5, 6, 7)
    ]
    for _, act in sorted(plan, key=lambda item: item[0]):
        act()
    for keep in keeps:
        keep.wait()
    outs += update(1)
    for offset in range(ZN):
        across_landed(offset, 0)
    outs += update(0)

    for out in outs:
        out.wait()
    beta.wait_send()
    for offset in range(1, RN):
        scatter(offset).wait_send()
        gather(offset).wait_send()
    for offset in range(ZN):
        for extra in range(2):
            across((z + offset) % ZN, extra).wait_send()
    for step in range(1, 9):
        for direction in range(2):
            for stream in STREAMS:
                if runs(direction, step, stream):
                    hop(direction, step, stream).wait_send()
    for hops in (0, REACH):
        for direction in range(2):
            for reach in x_far(direction, hops):
                x_hop(direction, hops, reach).wait_send()


def shards(rhs, panel_columns, diag_inverse, block_order):
    rows, width = rhs.shape
    piece = panel_columns.reshape(16, rows)
    bf16 = jnp.bfloat16
    dma = pltpu.SemaphoreType.DMA
    any_space = pl.BlockSpec(memory_space=pl.ANY)
    in_smem = pl.BlockSpec(memory_space=pltpu.SMEM)
    half = rows // 2
    span = width * 32 // RN
    return pl.pallas_call(
        whole,
        name="whole",
        out_shape=(
            jax.ShapeDtypeStruct((rows, width), bf16),
            jax.ShapeDtypeStruct((span, width), jnp.float32),
        ),
        in_specs=[in_smem, any_space, any_space, any_space],
        out_specs=(any_space, any_space),
        scratch_shapes=[
            pltpu.VMEM((rows, width), bf16),
            pltpu.VMEM((16, rows), bf16),
            pltpu.VMEM(diag_inverse.shape, jnp.float32),
            pltpu.VMEM((2, 2 * ZN, 16, half), bf16),
            pltpu.VMEM((2 * ZN, 80, 128), bf16),
            pltpu.VMEM((RN, 64, 128), bf16),
            pltpu.VMEM((RN, 80, 128), bf16),
            pltpu.VMEM((RN, 80, 128), bf16),
            pltpu.VMEM((80, 128), bf16),
            pltpu.VMEM((2, BLOCK, width), bf16),
            pltpu.VMEM((2 * BLOCK, width), bf16),
            pltpu.VMEM((rows, width), bf16),
            pltpu.VMEM((span, width), jnp.float32),
            dma((7,)), dma((RN,)), dma((RN,)), dma((RN,)), dma((RN,)), dma((2,)),
            dma((2, 9, 3)), dma((2, 9, 3)), dma((2,)), dma((ZN, 2)), dma((ZN, 2)),
            dma((2, 9)), dma((2, 9)), dma((2 * (half // TILE) + 1,)),
        ],
        compiler_params=pltpu.CompilerParams(
            collective_id=0, has_side_effects=True, vmem_limit_bytes=56 * 1024 * 1024
        ),
    )(block_order, diag_inverse, rhs, piece)


def solution(mesh):
    in_specs = (P("row", "col"), P(None, "col", "row"), P(), P())
    out_specs = (P("row", "col"), P("row", "col"))
    return jax.shard_map(shards, mesh=mesh, in_specs=in_specs, out_specs=out_specs, check_vma=False)
```

```python
import functools

import jax
import jax.numpy as jnp
from jax import lax
from jax.experimental import pallas as pl
from jax.experimental.pallas import tpu as pltpu
from jax.sharding import PartitionSpec as P

MESH = pl.DeviceIdType.MESH
BLOCK = 256
ZN = 16
RN = 16
NEAR, FAR, OTHER = STREAMS = range(3)
LAST = ((NEAR,), (FAR, OTHER))
STEP = 4.1
FIRST = {NEAR: 3.5, FAR: 4.5, OTHER: 6.0}
ADD_AT = 9.5
EXTRA_AT = 17.0
EXTRA_STEP = 4.5
SHARE_AT = 18.0
SOLVE_AT = 33.0
REACH = 3
TILE = 512


def split3(value):
    parts = []
    for _ in range(3):
        part = value.astype(jnp.bfloat16)
        parts.append(part)
        value = value - part.astype(jnp.float32)
    return parts


def times(matrix, value):
    return sum(jnp.dot(part, value, preferred_element_type=jnp.float32) for part in reversed(split3(matrix)))


def contract_rows(a, b):
    return lax.dot_general(a, b, (((0,), (0,)), ((), ())), preferred_element_type=jnp.float32)


def whole(
    order_ref, diag_ref, rhs_ref, piece_ref, work_ref, gram_ref,
    rhs_v, panel_v, diag_v, g_ref, x_ref, ag_ref, cand, pair, rs, total, solved, stacked, work_v, gram_v,
    local_sem, pair_sem, rs_send, rs_recv, ag_send, ag_recv, t_sem,
    g_send, g_recv, beta_sem, y_send, y_recv, x_send, x_recv, out_sem,
):
    row = lax.axis_index("row")
    col = lax.axis_index("col")
    ylo, z = col // ZN, col % ZN
    nblocks = rhs_ref.shape[0] // BLOCK
    width = g_ref.shape[3]
    local = pltpu.make_async_copy

    def at(r, c):
        return {"row": r, "col": c}

    def remote(src, dst, send, recv, device):
        return pltpu.make_async_remote_copy(
            src_ref=src, dst_ref=dst, send_sem=send, recv_sem=recv, device_id=device, device_id_type=MESH
        )

    core, chip = row % 2, row // 2

    def peer(offset):
        return at((chip + offset) % 8 * 2 + core, col)

    sibling = at(chip * 2 + 1 - core, col)

    lo_partner = at(row, (1 - ylo) * ZN + z)
    ring = (at(row, ylo * ZN + (z + 1) % ZN), at(row, ylo * ZN + (z + ZN - 1) % ZN))
    reaches = [
        (at(row, ylo * ZN + (z + far) % ZN), at(row, ylo * ZN + (z + ZN - far) % ZN)) for far in range(1, REACH + 1)
    ]
    t_row, t_col = col // 2, 2 * row + col % 2
    t_partner = at(t_row, t_col)
    t_self = jnp.logical_and(t_row == row, t_col == col)

    rhs_in = local(rhs_ref, rhs_v, local_sem.at[0])
    panel_in = local(piece_ref, panel_v, local_sem.at[1])
    rhs_in.start()
    panel_in.start()
    diag_in = local(diag_ref, diag_v, local_sem.at[6])
    diag_in.start()

    barrier = pltpu.get_barrier_semaphore()

    def greet(device):
        pl.semaphore_signal(barrier, inc=1, device_id=device, device_id_type=MESH)

    for offset in range(1, 8):
        greet(peer(offset))
    greet(sibling)
    greet(lo_partner)
    for both_ways in reaches:
        for device in both_ways:
            greet(device)

    @pl.when(jnp.logical_not(t_self))
    def _():
        greet(t_partner)

    pl.semaphore_wait(barrier, 9 + 2 * REACH + jnp.where(t_self, 0, 1))

    def origin(direction, hops):
        return (z + (ZN - hops if direction == 0 else hops)) % ZN

    def held(stream, place):
        plane = 1 - ylo if stream == OTHER else ylo
        return g_ref.at[0 if stream == NEAR else 1, plane * ZN + place]

    def own(stream):
        return piece_ref.at[:, pl.ds(stream * width, width)]

    def hop(direction, step, stream):
        dst = held(stream, origin(direction, step - 1))
        src = own(stream) if step == 1 and stream in (NEAR, FAR) else dst
        return remote(
            src, dst, g_send.at[direction, step, stream], g_recv.at[direction, step, stream], ring[direction]
        )

    def runs(direction, step, stream):
        return step < 8 or (step == 8 and stream in LAST[direction])

    def across(place, extra):
        place_in_col = ylo * ZN + place
        dst = x_ref.at[place_in_col] if extra else g_ref.at[0, place_in_col]
        offset = (place + ZN - z) % ZN
        return remote(dst, dst, y_send.at[offset, extra], y_recv.at[offset, extra], lo_partner)

    def across_landed(offset, extra):
        place_in_col = (1 - ylo) * ZN + (z + offset) % ZN
        dst = x_ref.at[place_in_col] if extra else g_ref.at[0, place_in_col]
        remote(dst, dst, y_send.at[offset, extra], y_recv.at[offset, extra], lo_partner).wait_recv()

    def begin(stream):
        for direction in range(2):
            hop(direction, 1, stream).start()

    def turn_over(step, stream):
        for direction in range(2):
            if not runs(direction, step, stream):
                continue
            place = origin(direction, step)
            dst = held(stream, place)
            remote(
                dst, dst, g_send.at[direction, step, stream], g_recv.at[direction, step, stream], ring[direction]
            ).wait_recv()
            if runs(direction, step + 1, stream):
                hop(direction, step + 1, stream).start()
            if stream == NEAR:
                across(place, 0).start()

    def x_far(direction, hops):
        return range(hops + 1, min(hops + REACH, 7 + (direction == 0)) + 1)

    def x_hop(direction, hops, reach):
        dst = x_ref.at[ylo * ZN + origin(direction, hops)]
        to = reaches[reach - hops - 1][direction]
        return remote(dst, dst, x_send.at[direction, reach], x_recv.at[direction, reach], to)

    def x_begin(hops):
        for reach in range(hops + REACH, hops, -1):
            for direction in range(2):
                if reach in x_far(direction, hops):
                    x_hop(direction, hops, reach).start()

    def x_landed(hops):
        for direction in range(2):
            if hops <= 7 + (direction == 0):
                dst = x_ref.at[ylo * ZN + origin(direction, hops)]
                remote(
                    dst, dst, x_send.at[direction, hops], x_recv.at[direction, hops], ring[direction]
                ).wait_recv()
                if hops in (REACH, 2 * REACH):
                    for reach in reversed(x_far(direction, hops)):
                        x_hop(direction, hops, reach).start()
                across(origin(direction, hops), 1).start()

    beta = remote(own(FAR), g_ref.at[1, ylo * ZN + z], beta_sem.at[0], beta_sem.at[1], lo_partner)
    beta.start()
    begin(NEAR)
    begin(FAR)
    remote(own(NEAR), held(NEAR, z), y_send.at[0, 0], y_recv.at[0, 0], lo_partner).start()

    rhs_in.wait()
    masks = [[(order_ref[row * nblocks + p] == b).astype(jnp.float32) for p in range(nblocks)] for b in range(2)]

    def masked(part, carry):
        for g in range(2):
            lanes = pl.ds(128 * g, 128)
            sums = [jnp.zeros((64, 128), jnp.float32)] * 2
            for p in range(nblocks):
                rows = pl.ds(pl.multiple_of(p * BLOCK + part * 64, 64), 64)
                value = rhs_v[rows, lanes].astype(jnp.float32)
                sums = [total_ + value * masks[b][p] for b, total_ in enumerate(sums)]
            for b in range(2):
                cand[part % 2 * 8 + g * 4 + b * 2 + part // 2, 0:64, :] = sums[b].astype(cand.dtype)
        return carry

    lax.fori_loop(0, 4, masked, 0)
    panel_in.wait()
    factor = jnp.zeros((8, BLOCK), jnp.float32)
    for p in range(nblocks):
        factor = factor + panel_v[:, pl.ds(p * BLOCK, BLOCK)].astype(jnp.float32)[0:8] * masks[1][p]
    factor = jnp.concatenate([factor[:, 0:128], factor[:, 128:256]], 0).astype(cand.dtype)
    for part in range(RN):
        cand[part, 64:80, :] = factor

    def side(ref, which):
        return ref.at[pl.ds(pl.multiple_of(which * 8, 8), 8)]

    halves = remote(side(cand, 1 - core), pair, pair_sem.at[0], pair_sem.at[1], sibling)
    halves.start()
    keeps = [local(own(stream), held(stream, z), local_sem.at[2 + stream]) for stream in (NEAR, FAR)]
    for keep in keeps:
        keep.start()

    theirs = held(OTHER, z)
    remote(theirs, theirs, beta_sem.at[0], beta_sem.at[1], lo_partner).wait_recv()
    begin(OTHER)

    def scatter(offset):
        return remote(
            pair.at[(chip + offset) % 8], rs.at[chip], rs_send.at[offset], rs_recv.at[offset], peer(offset)
        )

    halves.wait()
    for part in range(8):
        both = pair[part].astype(jnp.float32) + cand[core * 8 + part].astype(jnp.float32)
        pair[part] = both.astype(pair.dtype)
    for offset in range(1, 8):
        scatter(offset).start()
    rs[chip] = pair[chip]

    def gather(offset):
        return remote(
            total.at[pl.ds(0, 64)], ag_ref.at[core * 8 + chip], ag_send.at[offset], ag_recv.at[offset], peer(offset)
        )

    def slot(place):
        return x_ref.at[place, pl.ds(0, 64)]

    turn = remote(total.at[pl.ds(0, 64)], slot(t_col), t_sem.at[0], t_sem.at[1], t_partner)
    stay = local(total.at[pl.ds(0, 64)], slot(col), t_sem.at[0])
    corner = local(total.at[pl.ds(64, 16)], x_ref.at[col, pl.ds(64, 16)], local_sem.at[4])
    keep_slice = local(total.at[pl.ds(0, 64)], ag_ref.at[core * 8 + chip], local_sem.at[5])

    def add_up():
        for offset in range(1, 8):
            dst = rs.at[(chip + 8 - offset) % 8]
            remote(dst, dst, rs_send.at[offset], rs_recv.at[offset], lo_partner).wait_recv()
        summed = rs[0].astype(jnp.float32)
        for part in range(1, 8):
            summed = summed + rs[part].astype(jnp.float32)
        total[...] = summed.astype(total.dtype)

        @pl.when(t_self)
        def _():
            stay.start()

        @pl.when(jnp.logical_not(t_self))
        def _():
            turn.start()

        corner.start()
        for offset in range(1, 8):
            gather(offset).start()
        keep_slice.start()

    share = remote(side(ag_ref, core), side(ag_ref, core), pair_sem.at[2], pair_sem.at[3], sibling)

    def share_blocks():
        for offset in range(1, 8):
            dst = ag_ref.at[core * 8 + (chip + 8 - offset) % 8]
            remote(dst, dst, ag_send.at[offset], ag_recv.at[offset], lo_partner).wait_recv()
        keep_slice.wait()
        share.start()

    def begin_extra():
        @pl.when(t_self)
        def _():
            stay.wait()

        @pl.when(jnp.logical_not(t_self))
        def _():
            dst = slot(col)
            remote(dst, dst, t_sem.at[0], t_sem.at[1], t_partner).wait_recv()
            turn.wait_send()

        corner.wait()
        x_begin(0)
        across(z, 1).start()

    def solve():
        dst = side(ag_ref, 1 - core)
        remote(dst, dst, pair_sem.at[2], pair_sem.at[3], sibling).wait_recv()
        diag_in.wait()
        for offset in range(ZN):
            across_landed(offset, 1)

        def columns(b):
            sides = [jnp.concatenate([ag_ref[part % 2 * 8 + g * 4 + b * 2 + part // 2] for part in range(4)], 0) for g in range(2)]
            for parity in range(2):
                for g in range(2):
                    sides.append(
                        jnp.concatenate([x_ref[2 * (g * 8 + b * 4 + part) + parity, 0:64] for part in range(4)], 0)
                    )
            return jnp.concatenate(sides, 1)

        corner_rows = jnp.concatenate(
            [
                jnp.concatenate([x_ref[c, 64:80].astype(jnp.float32)[8 * g : 8 * g + 8] for c in range(2 * ZN)], 0)
                for g in range(2)
            ],
            1,
        ).astype(jnp.bfloat16)
        v0 = times(diag_v[0], columns(0)).astype(jnp.bfloat16)
        left = (columns(1).astype(jnp.float32) - contract_rows(corner_rows, v0)).astype(jnp.bfloat16)
        v1 = times(diag_v[1], left).astype(jnp.bfloat16)
        solved[0] = v0[:, 0:BLOCK]
        solved[1] = v1[:, 0:BLOCK]
        own0 = v0[:, 0:BLOCK].astype(jnp.float32).reshape(2 * ZN, 8, BLOCK)
        own1 = v1[:, 0:BLOCK].astype(jnp.float32).reshape(2 * ZN, 8, BLOCK)
        stacked[...] = jnp.concatenate([own0, own1], 1).reshape(2 * BLOCK, BLOCK).astype(jnp.bfloat16)
        everything = jnp.concatenate([v0[:, BLOCK:], v1[:, BLOCK:]], 0)
        finished = jnp.concatenate([v0[:, 0:BLOCK], v1[:, 0:BLOCK]], 0)
        gram_v[...] = contract_rows(everything, finished) / (2 * BLOCK)

    def update(half):
        outs = []
        for tile in range(width // TILE):
            panel = g_ref[half, :, :, pl.ds(tile * TILE, TILE)].reshape(2 * BLOCK, TILE)
            change = contract_rows(panel, stacked[...])
            for part in range(TILE // BLOCK):
                p = half * (width // BLOCK) + tile * (TILE // BLOCK) + part
                rows = pl.ds(p * BLOCK, BLOCK)
                fresh = rhs_v[rows, :].astype(jnp.float32) - change[part * BLOCK : (part + 1) * BLOCK]
                fresh = fresh.astype(jnp.bfloat16)
                which = order_ref[row * nblocks + p]
                fresh = jnp.where(which == 0, solved[0], fresh)
                work_v[rows, :] = jnp.where(which == 1, solved[1], fresh)
            rows = pl.ds(half * width + tile * TILE, TILE)
            out = local(work_v.at[rows], work_ref.at[rows], out_sem.at[half * (width // TILE) + tile])
            out.start()
            outs.append(out)
        return outs

    outs = []

    def solve_and_write():
        solve()
        out = local(gram_v, gram_ref, out_sem.at[2 * (width // TILE)])
        out.start()
        outs.append(out)

    plan = [
        (FIRST[stream] + STEP * (step - 1), functools.partial(turn_over, step, stream))
        for step in range(1, 9)
        for stream in STREAMS
    ]
    plan += [(SHARE_AT, share_blocks), (ADD_AT, add_up), (EXTRA_AT, begin_extra), (SOLVE_AT, solve_and_write)]
    plan += [
        (EXTRA_AT + EXTRA_STEP * (1 + (hops - 1) // REACH), functools.partial(x_landed, hops))
        for hops in (3, 1, 2, 6, 4, 5, 8, 7)
    ]
    for _, act in sorted(plan, key=lambda item: item[0]):
        act()
    for keep in keeps:
        keep.wait()
    outs += update(1)
    for offset in range(ZN):
        across_landed(offset, 0)
    outs += update(0)

    for out in outs:
        out.wait()
    beta.wait_send()
    share.wait_send()
    for offset in range(1, 8):
        scatter(offset).wait_send()
        gather(offset).wait_send()
    for offset in range(ZN):
        for extra in range(2):
            across((z + offset) % ZN, extra).wait_send()
    for step in range(1, 9):
        for direction in range(2):
            for stream in STREAMS:
                if runs(direction, step, stream):
                    hop(direction, step, stream).wait_send()
    for hops in (0, REACH, 2 * REACH):
        for direction in range(2):
            for reach in x_far(direction, hops):
                x_hop(direction, hops, reach).wait_send()


def deliver(work_ref, gram_ref, work_out, gram_out, work_v, gram_v, sem_in, sem_out):
    parts = work_ref.shape[0] // TILE
    ways = [(work_ref, work_v, work_out, pl.ds(i * TILE, TILE)) for i in range(parts)]
    ways.append((gram_ref, gram_v, gram_out, pl.ds(0, gram_ref.shape[0])))
    ins = [pltpu.make_async_copy(a.at[rows], v.at[rows], sem_in.at[i]) for i, (a, v, _, rows) in enumerate(ways)]
    outs = [pltpu.make_async_copy(v.at[rows], b.at[rows], sem_out.at[i]) for i, (_, v, b, rows) in enumerate(ways)]
    for copy in ins:
        copy.start()
    for copy, out in zip(ins, outs):
        copy.wait()
        out.start()
    for out in outs:
        out.wait()


def shards(rhs, panel_columns, diag_inverse, block_order):
    rows, width = rhs.shape
    piece = panel_columns.reshape(16, rows)
    bf16 = jnp.bfloat16
    dma = pltpu.SemaphoreType.DMA
    any_space = pl.BlockSpec(memory_space=pl.ANY)
    in_smem = pl.BlockSpec(memory_space=pltpu.SMEM)
    half = rows // 2
    span = width * 32 // RN
    work, gram = pl.pallas_call(
        whole,
        name="whole",
        out_shape=(
            jax.ShapeDtypeStruct((rows, width), bf16),
            jax.ShapeDtypeStruct((span, width), jnp.float32),
        ),
        in_specs=[in_smem, any_space, any_space, any_space],
        out_specs=(any_space, any_space),
        scratch_shapes=[
            pltpu.VMEM((rows, width), bf16),
            pltpu.VMEM((16, rows), bf16),
            pltpu.VMEM(diag_inverse.shape, jnp.float32),
            pltpu.VMEM((2, 2 * ZN, 16, half), bf16),
            pltpu.VMEM((2 * ZN, 80, 128), bf16),
            pltpu.VMEM((RN, 64, 128), bf16),
            pltpu.VMEM((RN, 80, 128), bf16),
            pltpu.VMEM((8, 80, 128), bf16),
            pltpu.VMEM((8, 80, 128), bf16),
            pltpu.VMEM((80, 128), bf16),
            pltpu.VMEM((2, BLOCK, width), bf16),
            pltpu.VMEM((2 * BLOCK, width), bf16),
            pltpu.VMEM((rows, width), bf16),
            pltpu.VMEM((span, width), jnp.float32),
            dma((7,)), dma((4,)), dma((8,)), dma((8,)), dma((8,)), dma((8,)), dma((2,)),
            dma((2, 9, 3)), dma((2, 9, 3)), dma((2,)), dma((ZN, 2)), dma((ZN, 2)),
            dma((2, 9)), dma((2, 9)), dma((2 * (half // TILE) + 1,)),
        ],
        compiler_params=pltpu.CompilerParams(
            collective_id=0, has_side_effects=True, vmem_limit_bytes=56 * 1024 * 1024
        ),
    )(block_order, diag_inverse, rhs, piece)
    return pl.pallas_call(
        deliver,
        name="deliver",
        out_shape=(
            jax.ShapeDtypeStruct((rows, width), bf16),
            jax.ShapeDtypeStruct((span, width), jnp.float32),
        ),
        in_specs=[any_space, any_space],
        out_specs=(any_space, any_space),
        scratch_shapes=[
            pltpu.VMEM((rows, width), bf16),
            pltpu.VMEM((span, width), jnp.float32),
            dma((rows // TILE + 1,)),
            dma((rows // TILE + 1,)),
        ],
        compiler_params=pltpu.CompilerParams(vmem_limit_bytes=60 * 1024 * 1024),
    )(work, gram)


def solution(mesh):
    in_specs = (P("row", "col"), P(None, "col", "row"), P(), P())
    out_specs = (P("row", "col"), P("row", "col"))
    return jax.shard_map(shards, mesh=mesh, in_specs=in_specs, out_specs=out_specs, check_vma=False)
```

```python
import functools

import jax
import jax.numpy as jnp
from jax import lax
from jax.experimental import pallas as pl
from jax.experimental.pallas import tpu as pltpu
from jax.sharding import PartitionSpec as P

MESH = pl.DeviceIdType.MESH
BLOCK = 256
ZN = 16
RN = 16
NEAR, FAR, OTHER = STREAMS = range(3)
LAST = ((NEAR,), (FAR, OTHER))
STEP = 4.1
FIRST = {NEAR: 3.5, FAR: 4.5, OTHER: 6.0}
ADD_AT = 9.5
EXTRA_AT = 17.0
EXTRA_STEP = 4.4
SHARE_AT = 18.0
SOLVE_AT = 37.0
REACH = 2
TILE = 512


def split3(value):
    parts = []
    for _ in range(3):
        part = value.astype(jnp.bfloat16)
        parts.append(part)
        value = value - part.astype(jnp.float32)
    return parts


def times(matrix, value):
    return sum(jnp.dot(part, value, preferred_element_type=jnp.float32) for part in reversed(split3(matrix)))


def contract_rows(a, b):
    return lax.dot_general(a, b, (((0,), (0,)), ((), ())), preferred_element_type=jnp.float32)


def whole(
    order_ref, diag_ref, rhs_ref, piece_ref, work_ref, gram_ref,
    rhs_v, panel_v, diag_v, g_ref, x_ref, ag_ref, cand, pair, rs, total, solved, stacked, work_v, gram_v,
    local_sem, pair_sem, rs_send, rs_recv, ag_send, ag_recv, t_sem,
    g_send, g_recv, beta_sem, y_send, y_recv, x_send, x_recv, out_sem,
):
    row = lax.axis_index("row")
    col = lax.axis_index("col")
    ylo, z = col // ZN, col % ZN
    nblocks = rhs_ref.shape[0] // BLOCK
    width = g_ref.shape[3]
    local = pltpu.make_async_copy

    def at(r, c):
        return {"row": r, "col": c}

    def remote(src, dst, send, recv, device):
        return pltpu.make_async_remote_copy(
            src_ref=src, dst_ref=dst, send_sem=send, recv_sem=recv, device_id=device, device_id_type=MESH
        )

    core, chip = row % 2, row // 2

    def peer(offset):
        return at((chip + offset) % 8 * 2 + core, col)

    sibling = at(chip * 2 + 1 - core, col)

    lo_partner = at(row, (1 - ylo) * ZN + z)
    ring = (at(row, ylo * ZN + (z + 1) % ZN), at(row, ylo * ZN + (z + ZN - 1) % ZN))
    reaches = [
        (at(row, ylo * ZN + (z + far) % ZN), at(row, ylo * ZN + (z + ZN - far) % ZN)) for far in range(1, REACH + 1)
    ]
    t_row, t_col = col // 2, 2 * row + col % 2
    t_partner = at(t_row, t_col)
    t_self = jnp.logical_and(t_row == row, t_col == col)

    rhs_in = local(rhs_ref, rhs_v, local_sem.at[0])
    panel_in = local(piece_ref, panel_v, local_sem.at[1])
    rhs_in.start()
    panel_in.start()
    diag_in = local(diag_ref, diag_v, local_sem.at[6])
    diag_in.start()

    barrier = pltpu.get_barrier_semaphore()

    def greet(device):
        pl.semaphore_signal(barrier, inc=1, device_id=device, device_id_type=MESH)

    for offset in range(1, 8):
        greet(peer(offset))
    greet(sibling)
    greet(lo_partner)
    for both_ways in reaches:
        for device in both_ways:
            greet(device)

    @pl.when(jnp.logical_not(t_self))
    def _():
        greet(t_partner)

    pl.semaphore_wait(barrier, 9 + 2 * REACH + jnp.where(t_self, 0, 1))

    def origin(direction, hops):
        return (z + (ZN - hops if direction == 0 else hops)) % ZN

    def held(stream, place):
        plane = 1 - ylo if stream == OTHER else ylo
        return g_ref.at[0 if stream == NEAR else 1, plane * ZN + place]

    def own(stream):
        return piece_ref.at[:, pl.ds(stream * width, width)]

    def hop(direction, step, stream):
        dst = held(stream, origin(direction, step - 1))
        src = own(stream) if step == 1 and stream in (NEAR, FAR) else dst
        return remote(
            src, dst, g_send.at[direction, step, stream], g_recv.at[direction, step, stream], ring[direction]
        )

    def runs(direction, step, stream):
        return step < 8 or (step == 8 and stream in LAST[direction])

    def across(place, extra):
        place_in_col = ylo * ZN + place
        dst = x_ref.at[place_in_col] if extra else g_ref.at[0, place_in_col]
        offset = (place + ZN - z) % ZN
        return remote(dst, dst, y_send.at[offset, extra], y_recv.at[offset, extra], lo_partner)

    def across_landed(offset, extra):
        place_in_col = (1 - ylo) * ZN + (z + offset) % ZN
        dst = x_ref.at[place_in_col] if extra else g_ref.at[0, place_in_col]
        remote(dst, dst, y_send.at[offset, extra], y_recv.at[offset, extra], lo_partner).wait_recv()

    def begin(stream):
        for direction in range(2):
            hop(direction, 1, stream).start()

    def turn_over(step, stream):
        for direction in range(2):
            if not runs(direction, step, stream):
                continue
            place = origin(direction, step)
            dst = held(stream, place)
            remote(
                dst, dst, g_send.at[direction, step, stream], g_recv.at[direction, step, stream], ring[direction]
            ).wait_recv()
            if runs(direction, step + 1, stream):
                hop(direction, step + 1, stream).start()
            if stream == NEAR:
                across(place, 0).start()

    def x_far(direction, hops):
        return range(hops + 1, min(hops + REACH, 7 + (direction == 0)) + 1)

    def x_hop(direction, hops, reach):
        dst = x_ref.at[ylo * ZN + origin(direction, hops)]
        to = reaches[reach - hops - 1][direction]
        return remote(dst, dst, x_send.at[direction, reach], x_recv.at[direction, reach], to)

    def x_begin(hops):
        for reach in range(hops + REACH, hops, -1):
            for direction in range(2):
                if reach in x_far(direction, hops):
                    x_hop(direction, hops, reach).start()

    def x_landed(hops):
        for direction in range(2):
            if hops <= 7 + (direction == 0):
                dst = x_ref.at[ylo * ZN + origin(direction, hops)]
                remote(
                    dst, dst, x_send.at[direction, hops], x_recv.at[direction, hops], ring[direction]
                ).wait_recv()
                if hops in (2, 4, 6):
                    for reach in reversed(x_far(direction, hops)):
                        x_hop(direction, hops, reach).start()
                across(origin(direction, hops), 1).start()

    beta = remote(own(FAR), g_ref.at[1, ylo * ZN + z], beta_sem.at[0], beta_sem.at[1], lo_partner)
    beta.start()
    begin(NEAR)
    begin(FAR)
    remote(own(NEAR), held(NEAR, z), y_send.at[0, 0], y_recv.at[0, 0], lo_partner).start()

    rhs_in.wait()
    masks = [[(order_ref[row * nblocks + p] == b).astype(jnp.float32) for p in range(nblocks)] for b in range(2)]

    def masked(part, carry):
        for g in range(2):
            lanes = pl.ds(128 * g, 128)
            sums = [jnp.zeros((64, 128), jnp.float32)] * 2
            for p in range(nblocks):
                rows = pl.ds(pl.multiple_of(p * BLOCK + part * 64, 64), 64)
                value = rhs_v[rows, lanes].astype(jnp.float32)
                sums = [total_ + value * masks[b][p] for b, total_ in enumerate(sums)]
            for b in range(2):
                cand[part % 2 * 8 + g * 4 + b * 2 + part // 2, 0:64, :] = sums[b].astype(cand.dtype)
        return carry

    lax.fori_loop(0, 4, masked, 0)
    panel_in.wait()
    factor = jnp.zeros((8, BLOCK), jnp.float32)
    for p in range(nblocks):
        factor = factor + panel_v[:, pl.ds(p * BLOCK, BLOCK)].astype(jnp.float32)[0:8] * masks[1][p]
    factor = jnp.concatenate([factor[:, 0:128], factor[:, 128:256]], 0).astype(cand.dtype)
    for part in range(RN):
        cand[part, 64:80, :] = factor

    def side(ref, which):
        return ref.at[pl.ds(pl.multiple_of(which * 8, 8), 8)]

    halves = remote(side(cand, 1 - core), pair, pair_sem.at[0], pair_sem.at[1], sibling)
    halves.start()
    keeps = [local(own(stream), held(stream, z), local_sem.at[2 + stream]) for stream in (NEAR, FAR)]
    for keep in keeps:
        keep.start()

    theirs = held(OTHER, z)
    remote(theirs, theirs, beta_sem.at[0], beta_sem.at[1], lo_partner).wait_recv()
    begin(OTHER)

    def scatter(offset):
        return remote(
            pair.at[(chip + offset) % 8], rs.at[chip], rs_send.at[offset], rs_recv.at[offset], peer(offset)
        )

    halves.wait()
    for part in range(8):
        both = pair[part].astype(jnp.float32) + cand[core * 8 + part].astype(jnp.float32)
        pair[part] = both.astype(pair.dtype)
    for offset in range(1, 8):
        scatter(offset).start()
    rs[chip] = pair[chip]

    def gather(offset):
        return remote(
            total.at[pl.ds(0, 64)], ag_ref.at[core * 8 + chip], ag_send.at[offset], ag_recv.at[offset], peer(offset)
        )

    def slot(place):
        return x_ref.at[place, pl.ds(0, 64)]

    turn = remote(total.at[pl.ds(0, 64)], slot(t_col), t_sem.at[0], t_sem.at[1], t_partner)
    stay = local(total.at[pl.ds(0, 64)], slot(col), t_sem.at[0])
    corner = local(total.at[pl.ds(64, 16)], x_ref.at[col, pl.ds(64, 16)], local_sem.at[4])
    keep_slice = local(total.at[pl.ds(0, 64)], ag_ref.at[core * 8 + chip], local_sem.at[5])

    def add_up():
        for offset in range(1, 8):
            dst = rs.at[(chip + 8 - offset) % 8]
            remote(dst, dst, rs_send.at[offset], rs_recv.at[offset], lo_partner).wait_recv()
        summed = rs[0].astype(jnp.float32)
        for part in range(1, 8):
            summed = summed + rs[part].astype(jnp.float32)
        total[...] = summed.astype(total.dtype)

        @pl.when(t_self)
        def _():
            stay.start()

        @pl.when(jnp.logical_not(t_self))
        def _():
            turn.start()

        corner.start()
        for offset in range(1, 8):
            gather(offset).start()
        keep_slice.start()

    share = remote(side(ag_ref, core), side(ag_ref, core), pair_sem.at[2], pair_sem.at[3], sibling)

    def share_blocks():
        for offset in range(1, 8):
            dst = ag_ref.at[core * 8 + (chip + 8 - offset) % 8]
            remote(dst, dst, ag_send.at[offset], ag_recv.at[offset], lo_partner).wait_recv()
        keep_slice.wait()
        share.start()

    def begin_extra():
        @pl.when(t_self)
        def _():
            stay.wait()

        @pl.when(jnp.logical_not(t_self))
        def _():
            dst = slot(col)
            remote(dst, dst, t_sem.at[0], t_sem.at[1], t_partner).wait_recv()
            turn.wait_send()

        corner.wait()
        x_begin(0)
        across(z, 1).start()

    def solve():
        dst = side(ag_ref, 1 - core)
        remote(dst, dst, pair_sem.at[2], pair_sem.at[3], sibling).wait_recv()
        diag_in.wait()
        for offset in range(ZN):
            across_landed(offset, 1)

        def columns(b):
            sides = [jnp.concatenate([ag_ref[part % 2 * 8 + g * 4 + b * 2 + part // 2] for part in range(4)], 0) for g in range(2)]
            for parity in range(2):
                for g in range(2):
                    sides.append(
                        jnp.concatenate([x_ref[2 * (g * 8 + b * 4 + part) + parity, 0:64] for part in range(4)], 0)
                    )
            return jnp.concatenate(sides, 1)

        corner_rows = jnp.concatenate(
            [
                jnp.concatenate([x_ref[c, 64:80].astype(jnp.float32)[8 * g : 8 * g + 8] for c in range(2 * ZN)], 0)
                for g in range(2)
            ],
            1,
        ).astype(jnp.bfloat16)
        v0 = times(diag_v[0], columns(0)).astype(jnp.bfloat16)
        left = (columns(1).astype(jnp.float32) - contract_rows(corner_rows, v0)).astype(jnp.bfloat16)
        v1 = times(diag_v[1], left).astype(jnp.bfloat16)
        solved[0] = v0[:, 0:BLOCK]
        solved[1] = v1[:, 0:BLOCK]
        own0 = v0[:, 0:BLOCK].astype(jnp.float32).reshape(2 * ZN, 8, BLOCK)
        own1 = v1[:, 0:BLOCK].astype(jnp.float32).reshape(2 * ZN, 8, BLOCK)
        stacked[...] = jnp.concatenate([own0, own1], 1).reshape(2 * BLOCK, BLOCK).astype(jnp.bfloat16)
        everything = jnp.concatenate([v0[:, BLOCK:], v1[:, BLOCK:]], 0)
        finished = jnp.concatenate([v0[:, 0:BLOCK], v1[:, 0:BLOCK]], 0)
        gram_v[...] = contract_rows(everything, finished) / (2 * BLOCK)

    def update(half):
        outs = []
        for tile in range(width // TILE):
            panel = g_ref[half, :, :, pl.ds(tile * TILE, TILE)].reshape(2 * BLOCK, TILE)
            change = contract_rows(panel, stacked[...])
            for part in range(TILE // BLOCK):
                p = half * (width // BLOCK) + tile * (TILE // BLOCK) + part
                rows = pl.ds(p * BLOCK, BLOCK)
                fresh = rhs_v[rows, :].astype(jnp.float32) - change[part * BLOCK : (part + 1) * BLOCK]
                fresh = fresh.astype(jnp.bfloat16)
                which = order_ref[row * nblocks + p]
                fresh = jnp.where(which == 0, solved[0], fresh)
                work_v[rows, :] = jnp.where(which == 1, solved[1], fresh)
            rows = pl.ds(half * width + tile * TILE, TILE)
            out = local(work_v.at[rows], work_ref.at[rows], out_sem.at[half * (width // TILE) + tile])
            out.start()
            outs.append(out)
        return outs

    outs = []

    def solve_and_write():
        solve()
        out = local(gram_v, gram_ref, out_sem.at[2 * (width // TILE)])
        out.start()
        outs.append(out)

    plan = [
        (FIRST[stream] + STEP * (step - 1), functools.partial(turn_over, step, stream))
        for step in range(1, 9)
        for stream in STREAMS
    ]
    plan += [(SHARE_AT, share_blocks), (ADD_AT, add_up), (EXTRA_AT, begin_extra), (SOLVE_AT, solve_and_write)]
    plan += [
        (EXTRA_AT + EXTRA_STEP * (1 + (hops - 1) // REACH), functools.partial(x_landed, hops))
        for hops in (2, 1, 4, 3, 6, 5, 8, 7)
    ]
    for _, act in sorted(plan, key=lambda item: item[0]):
        act()
    for keep in keeps:
        keep.wait()
    outs += update(1)
    for offset in range(ZN):
        across_landed(offset, 0)
    outs += update(0)

    for out in outs:
        out.wait()
    beta.wait_send()
    share.wait_send()
    for offset in range(1, 8):
        scatter(offset).wait_send()
        gather(offset).wait_send()
    for offset in range(ZN):
        for extra in range(2):
            across((z + offset) % ZN, extra).wait_send()
    for step in range(1, 9):
        for direction in range(2):
            for stream in STREAMS:
                if runs(direction, step, stream):
                    hop(direction, step, stream).wait_send()
    for hops in (0, 2, 4, 6):
        for direction in range(2):
            for reach in x_far(direction, hops):
                x_hop(direction, hops, reach).wait_send()


def deliver(work_ref, gram_ref, work_out, gram_out, work_v, gram_v, sem_in, sem_out):
    parts = work_ref.shape[0] // TILE
    ways = [(work_ref, work_v, work_out, pl.ds(i * TILE, TILE)) for i in range(parts)]
    ways.append((gram_ref, gram_v, gram_out, pl.ds(0, gram_ref.shape[0])))
    ins = [pltpu.make_async_copy(a.at[rows], v.at[rows], sem_in.at[i]) for i, (a, v, _, rows) in enumerate(ways)]
    outs = [pltpu.make_async_copy(v.at[rows], b.at[rows], sem_out.at[i]) for i, (_, v, b, rows) in enumerate(ways)]
    for copy in ins:
        copy.start()
    for copy, out in zip(ins, outs):
        copy.wait()
        out.start()
    for out in outs:
        out.wait()


def shards(rhs, panel_columns, diag_inverse, block_order):
    rows, width = rhs.shape
    piece = panel_columns.reshape(16, rows)
    bf16 = jnp.bfloat16
    dma = pltpu.SemaphoreType.DMA
    any_space = pl.BlockSpec(memory_space=pl.ANY)
    in_smem = pl.BlockSpec(memory_space=pltpu.SMEM)
    half = rows // 2
    span = width * 32 // RN
    work, gram = pl.pallas_call(
        whole,
        name="whole",
        out_shape=(
            jax.ShapeDtypeStruct((rows, width), bf16),
            jax.ShapeDtypeStruct((span, width), jnp.float32),
        ),
        in_specs=[in_smem, any_space, any_space, any_space],
        out_specs=(any_space, any_space),
        scratch_shapes=[
            pltpu.VMEM((rows, width), bf16),
            pltpu.VMEM((16, rows), bf16),
            pltpu.VMEM(diag_inverse.shape, jnp.float32),
            pltpu.VMEM((2, 2 * ZN, 16, half), bf16),
            pltpu.VMEM((2 * ZN, 80, 128), bf16),
            pltpu.VMEM((RN, 64, 128), bf16),
            pltpu.VMEM((RN, 80, 128), bf16),
            pltpu.VMEM((8, 80, 128), bf16),
            pltpu.VMEM((8, 80, 128), bf16),
            pltpu.VMEM((80, 128), bf16),
            pltpu.VMEM((2, BLOCK, width), bf16),
            pltpu.VMEM((2 * BLOCK, width), bf16),
            pltpu.VMEM((rows, width), bf16),
            pltpu.VMEM((span, width), jnp.float32),
            dma((7,)), dma((4,)), dma((8,)), dma((8,)), dma((8,)), dma((8,)), dma((2,)),
            dma((2, 9, 3)), dma((2, 9, 3)), dma((2,)), dma((ZN, 2)), dma((ZN, 2)),
            dma((2, 9)), dma((2, 9)), dma((2 * (half // TILE) + 1,)),
        ],
        compiler_params=pltpu.CompilerParams(
            collective_id=0, has_side_effects=True, vmem_limit_bytes=56 * 1024 * 1024
        ),
    )(block_order, diag_inverse, rhs, piece)
    return pl.pallas_call(
        deliver,
        name="deliver",
        out_shape=(
            jax.ShapeDtypeStruct((rows, width), bf16),
            jax.ShapeDtypeStruct((span, width), jnp.float32),
        ),
        in_specs=[any_space, any_space],
        out_specs=(any_space, any_space),
        scratch_shapes=[
            pltpu.VMEM((rows, width), bf16),
            pltpu.VMEM((span, width), jnp.float32),
            dma((rows // TILE + 1,)),
            dma((rows // TILE + 1,)),
        ],
        compiler_params=pltpu.CompilerParams(vmem_limit_bytes=60 * 1024 * 1024),
    )(work, gram)


def solution(mesh):
    in_specs = (P("row", "col"), P(None, "col", "row"), P(), P())
    out_specs = (P("row", "col"), P("row", "col"))
    return jax.shard_map(shards, mesh=mesh, in_specs=in_specs, out_specs=out_specs, check_vma=False)
```
